512 devices in a mesh: tensor: 16 (over y_hi, x, core), context: 32 (over y_lo, z).
Axes of the slice: x: 4, y: 8 (y_hi: 2, y_lo: 4; y = y_hi * 4 + y_lo), z: 8, core: 2. Of those that a mesh axis runs over, the one named last changes fastest.
Arguments:
- values: bfloat16 [32768, 2048], P('context', 'tensor'), may hold values from -6 to 6
- long_filter: bfloat16 [32768, 2048], P('context', 'tensor'), may hold values from -0.03125 to 0.03125
- skip_gain: float32 [2048], P('tensor'), may hold values from -3 to 3
Outputs:
- layer_out: bfloat16 [32768, 2048], P('context', 'tensor')
The draws below stay inside these ranges and needn't reach their ends.
All inputs are finite; a program needn't handle non-finite values.
Results may differ from the reference program's by a relative error of at most 0.011.
Values may be sent and summed in bfloat16 or wider, within the bound.
A program may use at most 64 MiB of HBM per device.

```python
import math
import jax
import jax.numpy as jnp
from jax import lax

CH = 2048
SEQ = 32768
F1 = 32
N_TENSOR = 16
N_CONTEXT = 32


def block_levels(stream_key, shape, cuts, low, high):
    loudness, own = 1.0, jax.random.fold_in(stream_key, 6)
    for axis_at, blocks in cuts:
        draws = jnp.exp(jax.random.uniform(jax.random.fold_in(own, axis_at), (blocks,), jnp.float32, low / len(cuts), high / len(cuts)))
        loudness = loudness * jnp.repeat(draws, shape[axis_at] // blocks).reshape([-1 if axis == axis_at else 1 for axis in range(len(shape))])
    return loudness


def centred(key, extent, width, most, pieces=(), kind=jnp.bfloat16):
    level = block_levels(key, extent, pieces, -0.22, 0.18) if pieces else 1.0
    values = jax.random.normal(key, extent, jnp.float32) * width * level
    return jnp.minimum(jnp.maximum(values, -most), most).astype(kind)


def setup_inputs(seed: int = 0) -> dict:
    seeds = jax.random.split(jax.random.key(seed), 4)
    return {
        "values": centred(seeds[0], (SEQ, CH), 1.0, 6.0, ((0, 32), (1, 16))),
        "long_filter": centred(seeds[1], (SEQ, CH), SEQ ** -0.5, 0.03125, ((0, 32), (1, 16))),
        "skip_gain": centred(seeds[2], (CH,), 0.5, 3.0, ((0, 16),), jnp.float32),
    }


TWO_PI = 2.0 * math.pi


def dft_rows(length, sign_value):
    index_vals = jnp.arange(length, dtype=jnp.int32)
    product = (index_vals[:, None] * index_vals[None, :]) % length
    angles = (TWO_PI / length) * product.astype(jnp.float32)
    cosine = jnp.cos(angles)
    sine_part = sign_value * jnp.sin(angles)
    upper_rows = jnp.stack([cosine, -sine_part], axis=1)
    lower_rows = jnp.stack([sine_part, cosine], axis=1)
    return jnp.stack([upper_rows, lower_rows], axis=0).astype(jnp.bfloat16)


def column_rows(column_count, factor, sign_value):
    index_vals = jnp.arange(column_count, dtype=jnp.int32)
    product = (index_vals[:, None] * index_vals[None, :]) % (2 * column_count)
    angles = (TWO_PI / (2 * column_count)) * product.astype(jnp.float32)
    parity = 1.0 - 2.0 * (index_vals % 2).astype(jnp.float32)
    is_first = (index_vals == 0)[None, :]
    real_rows = jnp.where(is_first, 1.0, factor * jnp.cos(angles))
    imag_rows = jnp.where(is_first, parity[:, None], factor * sign_value * jnp.sin(angles))
    return jnp.stack([real_rows, imag_rows], axis=2).astype(jnp.bfloat16)


def complex_product(left_re, left_im, right_re, right_im):
    return left_re * right_re - left_im * right_im, left_re * right_im + left_im * right_re


def pack_lanes(real_part, imag_part, columns):
    half_lanes = real_part.shape[-1] // 2
    packed_re = jnp.concatenate([real_part[..., :half_lanes], imag_part[..., :half_lanes]], axis=-1)
    packed_im = jnp.concatenate([real_part[..., half_lanes:], imag_part[..., half_lanes:]], axis=-1)
    is_first = (columns == 0).reshape((-1,) + (1,) * (real_part.ndim - 1))
    return jnp.where(is_first, packed_re, real_part), jnp.where(is_first, packed_im, imag_part)


def position_grid(a_start, a_count, b_start, b_count, b_total):
    a_vals = a_start + jnp.arange(a_count, dtype=jnp.int32)
    b_vals = b_start + jnp.arange(b_count, dtype=jnp.int32)
    return a_vals[:, None] * b_total + b_vals[None, :]


def column_twiddle(columns, position, lane_count, column_count, length, sign_value):
    lane_index = jnp.arange(lane_count, dtype=jnp.int32)
    column = columns.reshape(-1, 1, 1, 1)
    exponent = jnp.where(column == 0, jnp.where(lane_index >= lane_count // 2, column_count, 0), column)
    product = (position[None, :, :, None] * exponent) % length
    angles = (sign_value * TWO_PI / length) * product.astype(jnp.float32)
    return jnp.cos(angles), jnp.sin(angles)


def row_twiddle(b_start, b_count, row_total, sign_value):
    s_vals = jnp.arange(F1, dtype=jnp.int32)
    b_vals = b_start + jnp.arange(b_count, dtype=jnp.int32)
    product = (s_vals[:, None] * b_vals[None, :]) % row_total
    angles = (sign_value * TWO_PI / row_total) * product.astype(jnp.float32)
    return jnp.cos(angles)[None, :, :, None], jnp.sin(angles)[None, :, :, None]


def first_columns(blocks, table_a, columns, position, column_count, length):
    summed = jnp.einsum("cql,cabh->qlabh", table_a.astype(jnp.float32), blocks.astype(jnp.float32))
    real_part, imag_part = pack_lanes(summed[:, 0], summed[:, 1], columns)
    cos_part, sin_part = column_twiddle(columns, position, blocks.shape[-1], column_count, length, -1.0)
    real_part, imag_part = complex_product(real_part, imag_part, cos_part, sin_part)
    return jnp.stack([real_part, imag_part], axis=1).astype(jnp.bfloat16)


def section_one(blocks, twiddle):
    summed = jnp.einsum("osia,qiabh->qosbh", dft_rows(F1, -1.0).astype(jnp.float32), blocks.astype(jnp.float32))
    real_part, imag_part = complex_product(summed[:, 0], summed[:, 1], twiddle[0], twiddle[1])
    return jnp.stack([real_part, imag_part], axis=1).astype(jnp.bfloat16)


def section_two(blocks):
    f_two = blocks.shape[3]
    summed = jnp.einsum("otib,qisbh->qotsh", dft_rows(f_two, -1.0).astype(jnp.float32), blocks.astype(jnp.float32))
    return summed.reshape(summed.shape[0], 2, f_two * F1, summed.shape[-1])


def back_two(blocks, twiddle):
    f_two = blocks.shape[2] // F1
    shaped = blocks.reshape(blocks.shape[0], 2, f_two, F1, blocks.shape[-1])
    summed = jnp.einsum("obit,qitsh->qosbh", dft_rows(f_two, 1.0).astype(jnp.float32), shaped.astype(jnp.float32))
    real_part, imag_part = complex_product(summed[:, 0], summed[:, 1], twiddle[0], twiddle[1])
    return jnp.stack([real_part, imag_part], axis=1).astype(jnp.bfloat16)


def back_one(blocks, columns, position, column_count, length):
    summed = jnp.einsum("oais,qisbh->qoabh", dft_rows(F1, 1.0).astype(jnp.float32), blocks.astype(jnp.float32))
    cos_part, sin_part = column_twiddle(columns, position, blocks.shape[-1], column_count, length, 1.0)
    real_part, imag_part = complex_product(summed[:, 0], summed[:, 1], cos_part, sin_part)
    return jnp.stack([real_part, imag_part], axis=1).astype(jnp.bfloat16)


def last_rows(blocks, table_b, columns, length):
    real_part, imag_part = pack_lanes(blocks[:, 0], blocks[:, 1], columns)
    packed = jnp.stack([real_part, imag_part], axis=1)
    summed = jnp.einsum("cql,qlabh->cabh", table_b.astype(jnp.float32), packed.astype(jnp.float32))
    return (summed * (1.0 / length)).astype(jnp.bfloat16)


def mirror_conj(part_re, part_im):
    lane_count = part_re.shape[-1]
    lane_index = jnp.arange(lane_count, dtype=jnp.int32)[None, :]
    flip_re = jnp.flip(part_re, axis=0)
    flip_im = jnp.flip(part_im, axis=0)
    mirror_re = jnp.where(lane_index < lane_count // 2, jnp.roll(flip_re, 1, axis=0), flip_re)
    mirror_im = -jnp.where(lane_index < lane_count // 2, jnp.roll(flip_im, 1, axis=0), flip_im)
    return mirror_re, mirror_im


def apply_filter(spec_re, spec_im, filt_re, filt_im, column):
    def plain_column(operand):
        return complex_product(spec_re, spec_im, filt_re, filt_im)

    def paired_column(operand):
        other_re, other_im = mirror_conj(filt_re, filt_im)
        plus_re = 0.25 * (filt_re + filt_im + other_re - other_im)
        plus_im = 0.25 * (filt_im - filt_re + other_im + other_re)
        minus_re = 0.25 * (filt_re - filt_im + other_re + other_im)
        minus_im = 0.25 * (filt_im + filt_re + other_im - other_re)
        mirror_re, mirror_im = mirror_conj(spec_re, spec_im)
        own_re, own_im = complex_product(spec_re, spec_im, plus_re, plus_im)
        side_re, side_im = complex_product(mirror_re, mirror_im, minus_re, minus_im)
        return own_re + side_re, own_im + side_im

    return lax.cond(column == 0, paired_column, plain_column, 0)


def reference(values, long_filter, skip_gain):
    column_count = N_CONTEXT
    tok_dev = SEQ // N_CONTEXT
    f_two = tok_dev // F1
    length = 2 * SEQ
    lane_count = CH // N_TENSOR
    table_a = column_rows(column_count, 1.0, -1.0)
    table_b = column_rows(column_count, 2.0, -1.0)
    columns = jnp.arange(column_count, dtype=jnp.int32)
    position = position_grid(0, F1, 0, f_two, f_two)
    twiddle_fwd = row_twiddle(0, f_two, tok_dev, -1.0)
    twiddle_back = row_twiddle(0, f_two, tok_dev, 1.0)

    def forward(group_data):
        blocks = group_data.reshape(column_count, F1, f_two, lane_count)
        twisted = first_columns(blocks, table_a, columns, position, column_count, length)
        return section_two(section_one(twisted, twiddle_fwd))

    def one_group(operands):
        group_values, group_filter = operands
        spectrum = forward(group_values)
        filter_spec = forward(group_filter)

        def one_column(item):
            column, spec_re, spec_im, filt_re, filt_im = item
            out_re, out_im = apply_filter(spec_re, spec_im, filt_re, filt_im, column)
            return jnp.stack([out_re, out_im], axis=0).astype(jnp.bfloat16)

        filtered = lax.map(one_column, (columns, spectrum[:, 0], spectrum[:, 1], filter_spec[:, 0], filter_spec[:, 1]))
        back_half = back_two(filtered, twiddle_back)
        returned = back_one(back_half, columns, position, column_count, length)
        convolved = last_rows(returned, table_b, columns, length)
        return convolved.reshape(SEQ, lane_count)

    grouped = (values.reshape(SEQ, N_TENSOR, lane_count).transpose(1, 0, 2),
               long_filter.reshape(SEQ, N_TENSOR, lane_count).transpose(1, 0, 2))
    convolved = lax.map(one_group, grouped).transpose(1, 0, 2).reshape(SEQ, CH)
    return (convolved.astype(jnp.float32) + skip_gain[None, :] * values.astype(jnp.float32)).astype(jnp.bfloat16)
```

```python
import math

import jax
import jax.numpy as jnp
import ml_dtypes
import numpy as np
from jax import lax
from jax.experimental import pallas as pl
from jax.experimental.pallas import tpu as pltpu
from jax.sharding import PartitionSpec as P

MESH = pl.DeviceIdType.MESH

N_DEV = 32
BLOCK = 1024
OWN = 4
HIGH, LOW = 8, 128
L1, L2 = 512, 128
N1 = L1 // 2
K1 = 272


def tables():
    length = L1 * L2
    k1 = np.arange(K1)
    n1 = np.arange(N1)
    n2 = np.arange(L2)
    kept = (k1 <= N1).astype(np.float64)[:, None]
    angle = 2 * math.pi * ((k1[:, None] * n1[None, :]) % L1) / L1
    first = np.concatenate([np.cos(angle) * kept, -np.sin(angle) * kept], axis=0)
    twist = 2 * math.pi * ((k1[:, None] * n2[None, :]) % length) / length
    angle = 2 * math.pi * ((n2[:, None] * n2[None, :]) % L2) / L2
    cosine, sine = np.cos(angle), np.sin(angle)
    second = np.block([[cosine, -sine], [sine, cosine]])
    back = np.block([[cosine, sine], [-sine, cosine]])
    k1 = np.arange(N1)
    angle = 2 * math.pi * ((n1[:, None] * k1[None, :]) % L1) / L1
    real = np.where(k1 == 0, 1.0, 2.0)[None, :] * np.cos(angle)
    imag = np.where(k1 == 0, (1.0 - 2.0 * (n1 % 2))[:, None], -2.0 * np.sin(angle))
    last = np.concatenate([real, imag], axis=1) / length
    half = ml_dtypes.bfloat16
    return (
        first.astype(half),
        np.cos(twist).astype(np.float32),
        np.sin(twist).astype(np.float32),
        second.astype(half),
        back.astype(half),
        last.astype(half),
    )


def dot(left, right):
    return jnp.dot(left, right, preferred_element_type=jnp.float32)


def kernel(
    values_ref,
    filter_ref,
    gain_ref,
    first_ref,
    cos_ref,
    sin_ref,
    second_ref,
    back_ref,
    last_ref,
    out_ref,
    wide,
    send,
    recv,
    line,
    spec,
    send_sem,
    recv_sem,
):
    me = lax.axis_index("context")
    barrier = pltpu.get_barrier_semaphore()

    def greet(k, carry):
        pl.semaphore_signal(
            barrier, inc=1, device_id={"context": lax.rem(me + k, N_DEV)}, device_id_type=MESH
        )
        return carry

    lax.fori_loop(1, N_DEV, greet, 0)

    def pack(source, slot):
        for high in range(HIGH):
            turned = source[high * LOW : (high + 1) * LOW, :].astype(jnp.float32).T
            for own in range(OWN):
                wide[own % 2, pl.ds((own // 2) * HIGH + high, N_DEV, stride=2 * HIGH), :] = turned[
                    own * N_DEV : (own + 1) * N_DEV, :
                ]
        for lower in range(2):
            send[slot, :, :, lower * LOW : (lower + 1) * LOW] = (
                wide[lower].astype(jnp.bfloat16).reshape(N_DEV, 2 * HIGH, LOW)
            )
        recv[slot, me] = send[slot, me]

    def copy_to(slot, device):
        return pltpu.make_async_remote_copy(
            src_ref=send.at[slot, device],
            dst_ref=recv.at[slot, me],
            send_sem=send_sem.at[slot],
            recv_sem=recv_sem.at[slot],
            device_id={"context": device},
            device_id_type=MESH,
        )

    def send_all(slot):
        def step(k, carry):
            copy_to(slot, lax.rem(me + k, N_DEV)).start()
            return carry

        lax.fori_loop(1, N_DEV, step, 0)

    def wait_all(buffer, slot, sem):
        blocks = buffer.at[slot, pl.ds(0, N_DEV - 1)]
        pltpu.make_async_copy(blocks, blocks, sem.at[slot]).wait()

    def spectrum(slot):
        rows = recv[slot].reshape(N_DEV * 2 * HIGH, 2 * LOW).astype(jnp.float32)
        rows = rows.reshape(N_DEV, 2, HIGH, 2 * LOW)
        for upper in range(2):
            part = rows[:, upper].reshape(N1, 2 * LOW).astype(jnp.bfloat16)
            summed = dot(first_ref[...], part)
            for lower in range(2):
                own = 2 * upper + lower
                real = summed[:K1, lower * LOW : (lower + 1) * LOW]
                imag = summed[K1:, lower * LOW : (lower + 1) * LOW]
                cosine, sine = cos_ref[...], sin_ref[...]
                line[own * K1 : (own + 1) * K1, :LOW] = (real * cosine + imag * sine).astype(
                    jnp.bfloat16
                )
                line[own * K1 : (own + 1) * K1, LOW:] = (imag * cosine - real * sine).astype(
                    jnp.bfloat16
                )
        return dot(line[...], second_ref[...])

    pack(filter_ref, 0)
    pl.semaphore_wait(barrier, N_DEV - 1)
    send_all(0)
    pack(values_ref, 1)
    send_all(1)

    wait_all(recv, 0, recv_sem)
    spec[...] = spectrum(0)
    wait_all(recv, 1, recv_sem)
    values_spec = spectrum(1)

    left_re, left_im = values_spec[:, :LOW], values_spec[:, LOW:]
    right_re, right_im = spec[:, :LOW], spec[:, LOW:]
    line[:, :LOW] = (left_re * right_re - left_im * right_im).astype(jnp.bfloat16)
    line[:, LOW:] = (left_re * right_im + left_im * right_re).astype(jnp.bfloat16)
    spec[...] = dot(line[...], back_ref[...])
    for upper in range(2):
        halves = []
        for lower in range(2):
            own = 2 * upper + lower
            real = spec[own * K1 : (own + 1) * K1, :LOW]
            imag = spec[own * K1 : (own + 1) * K1, LOW:]
            cosine, sine = cos_ref[...], sin_ref[...]
            turned_re = real * cosine - imag * sine
            turned_im = (imag * cosine + real * sine)[:N1]
            row = lax.broadcasted_iota(jnp.int32, (N1, LOW), 0)
            turned_im = jnp.where(row == 0, turned_re[N1 : N1 + 1], turned_im)
            halves.append(
                jnp.concatenate([turned_re[:N1], turned_im], axis=0).astype(jnp.bfloat16)
            )
        result = dot(last_ref[...], jnp.concatenate(halves, axis=1))
        result = result.reshape(N_DEV, HIGH, 2 * LOW)
        for device in range(N_DEV):
            start = device * 2 * HIGH + upper * HIGH
            for lower in range(2):
                wide[lower, start : start + HIGH, :] = result[
                    device, :, lower * LOW : (lower + 1) * LOW
                ]
    for lower in range(2):
        send[2, :, :, lower * LOW : (lower + 1) * LOW] = (
            wide[lower].astype(jnp.bfloat16).reshape(N_DEV, 2 * HIGH, LOW)
        )
    recv[2, me] = send[2, me]
    send_all(2)
    wait_all(recv, 2, recv_sem)
    for lower in range(2):
        wide[lower] = (
            recv[2, :, :, lower * LOW : (lower + 1) * LOW]
            .reshape(N_DEV * 2 * HIGH, LOW)
            .astype(jnp.float32)
        )
    for high in range(HIGH):
        turned = jnp.concatenate(
            [
                wide[own % 2, pl.ds((own // 2) * HIGH + high, N_DEV, stride=2 * HIGH), :]
                for own in range(OWN)
            ],
            axis=0,
        ).T
        direct = gain_ref[...] * values_ref[high * LOW : (high + 1) * LOW, :].astype(jnp.float32)
        out_ref[high * LOW : (high + 1) * LOW, :] = (turned + direct).astype(jnp.bfloat16)
    for slot in range(3):
        wait_all(send, slot, send_sem)


def body(values, long_filter, skip_gain):
    lanes = values.shape[1]
    vmem = pl.BlockSpec(memory_space=pltpu.VMEM)
    return pl.pallas_call(
        kernel,
        out_shape=jax.ShapeDtypeStruct(values.shape, jnp.bfloat16),
        in_specs=[vmem] * 9,
        out_specs=vmem,
        scratch_shapes=[
            pltpu.VMEM((2, N_DEV * 2 * HIGH, LOW), jnp.float32),
            pltpu.VMEM((3, N_DEV, 2 * HIGH, 2 * LOW), jnp.bfloat16),
            pltpu.VMEM((3, N_DEV, 2 * HIGH, 2 * LOW), jnp.bfloat16),
            pltpu.VMEM((OWN * K1, 2 * LOW), jnp.bfloat16),
            pltpu.VMEM((OWN * K1, 2 * LOW), jnp.float32),
            pltpu.SemaphoreType.DMA((3,)),
            pltpu.SemaphoreType.DMA((3,)),
        ],
        compiler_params=pltpu.CompilerParams(
            collective_id=0, has_side_effects=True, vmem_limit_bytes=40 * 2**20
        ),
    )(values, long_filter, skip_gain.reshape(1, lanes), *(jnp.asarray(t) for t in tables()))


def solution(mesh):
    return jax.shard_map(
        body,
        mesh=mesh,
        in_specs=(P("context", "tensor"), P("context", "tensor"), P("tensor")),
        out_specs=P("context", "tensor"),
        check_vma=False,
    )
```

```python
import math

import jax
import jax.numpy as jnp
import ml_dtypes
import numpy as np
from jax import lax
from jax.experimental import pallas as pl
from jax.experimental.pallas import tpu as pltpu
from jax.sharding import PartitionSpec as P

MESH = pl.DeviceIdType.MESH

N_DEV = 32
BLOCK = 1024
OWN = 4
HIGH, LOW = 8, 128
L1, L2 = 512, 128
N1 = L1 // 2
K1 = 272


def tables():
    length = L1 * L2
    k1 = np.arange(K1)
    n1 = np.arange(N1)
    n2 = np.arange(L2)
    kept = (k1 <= N1).astype(np.float64)[:, None]
    angle = 2 * math.pi * ((k1[:, None] * n1[None, :]) % L1) / L1
    first = np.concatenate([np.cos(angle) * kept, -np.sin(angle) * kept], axis=0)
    twist = 2 * math.pi * ((k1[:, None] * n2[None, :]) % length) / length
    angle = 2 * math.pi * ((n2[:, None] * n2[None, :]) % L2) / L2
    cosine, sine = np.cos(angle), np.sin(angle)
    second = np.block([[cosine, -sine], [sine, cosine]])
    back = np.block([[cosine, sine], [-sine, cosine]])
    k1 = np.arange(N1)
    angle = 2 * math.pi * ((n1[:, None] * k1[None, :]) % L1) / L1
    real = np.where(k1 == 0, 1.0, 2.0)[None, :] * np.cos(angle)
    imag = np.where(k1 == 0, (1.0 - 2.0 * (n1 % 2))[:, None], -2.0 * np.sin(angle))
    last = np.concatenate([real, imag], axis=1) / length
    matrices = np.concatenate([first, second, back, last[:, :N1], last[:, N1:]], axis=0)
    twists = np.concatenate([np.cos(twist), np.sin(twist)], axis=0)
    return matrices.astype(ml_dtypes.bfloat16), twists.astype(np.float32)


def dot(left, right):
    return jnp.dot(left, right, preferred_element_type=jnp.float32)


def partner(me, k):
    turn, along_y = k // 4, lax.rem(k + 1, 4)
    along_z = 4 + (1 - 2 * lax.rem(turn, 2)) * ((turn + 1) // 2)
    y, z = me // 8, lax.rem(me, 8)
    return lax.rem(y + along_y, 4) * 8 + lax.rem(z + along_z, 8)


def kernel(
    filter_hbm,
    values_hbm,
    matrices_hbm,
    twists_hbm,
    out_ref,
    filter_ref,
    values_ref,
    matrices_ref,
    twists_ref,
    load_sem,
    wide,
    send_in,
    recv_in,
    send_out,
    recv_out,
    line,
    spec,
    send_sem,
    recv_sem,
):
    me = lax.axis_index("context")
    barrier = pltpu.get_barrier_semaphore()
    pairs = [
        (filter_hbm, filter_ref),
        (values_hbm, values_ref),
        (matrices_hbm, matrices_ref),
        (twists_hbm, twists_ref),
    ]
    loads = [
        pltpu.make_async_copy(source, target, load_sem.at[i])
        for i, (source, target) in enumerate(pairs)
    ]
    for load in loads:
        load.start()
    for k in range(N_DEV - 1):
        pl.semaphore_signal(
            barrier, inc=1, device_id={"context": partner(me, k)}, device_id_type=MESH
        )

    rows = [0, 2 * K1, 2 * K1 + 2 * LOW, 2 * K1 + 4 * LOW, 2 * K1 + 4 * LOW + N1]
    first, second, back, last_re, last_im = (
        matrices_ref.at[pl.ds(start, size)]
        for start, size in zip(rows, [2 * K1, 2 * LOW, 2 * LOW, N1, N1])
    )
    cos_ref, sin_ref = twists_ref.at[pl.ds(0, K1)], twists_ref.at[pl.ds(K1, K1)]

    def pack(source, lanes):
        for high in range(HIGH):
            turned = source[high * LOW : (high + 1) * LOW, :].astype(jnp.float32).T
            for own in range(OWN):
                wide[own // 2, pl.ds((own % 2) * HIGH + high, N_DEV, stride=2 * HIGH), :] = turned[
                    own * N_DEV : (own + 1) * N_DEV, :
                ]
        for half in range(2):
            send_in[half, :, :, lanes : lanes + LOW] = (
                wide[half].astype(jnp.bfloat16).reshape(N_DEV, 2 * HIGH, LOW)
            )

    def send_all(source, target, half, sem):
        def step(k, carry):
            device = partner(me, k)
            pltpu.make_async_remote_copy(
                src_ref=source.at[half, device],
                dst_ref=target.at[half, me],
                send_sem=send_sem.at[sem],
                recv_sem=recv_sem.at[sem],
                device_id={"context": device},
                device_id_type=MESH,
            ).start()
            return carry

        lax.fori_loop(0, N_DEV - 1, step, 0)
        target[half, me] = source[half, me]

    def wait_all(buffer, half, sem):
        blocks = buffer.at[half, pl.ds(0, N_DEV - 1)]
        pltpu.make_async_copy(blocks, blocks, sem).wait()

    def convolve(half):
        rows = recv_in[half].reshape(N_DEV * 2 * HIGH, 2 * LOW).astype(jnp.float32)
        rows = rows.reshape(N_DEV, 2, HIGH, 2 * LOW)
        cosine, sine = cos_ref[...], sin_ref[...]
        for own in range(2):
            part = rows[:, own].reshape(N1, 2 * LOW).astype(jnp.bfloat16)
            summed = dot(first[...], part)
            for array in range(2):
                start = (2 * array + own) * K1
                real = summed[:K1, array * LOW : (array + 1) * LOW]
                imag = summed[K1:, array * LOW : (array + 1) * LOW]
                line[start : start + K1, :LOW] = (real * cosine + imag * sine).astype(jnp.bfloat16)
                line[start : start + K1, LOW:] = (imag * cosine - real * sine).astype(jnp.bfloat16)
        spec[...] = dot(line[...], second[...])
        left_re, left_im = spec[: 2 * K1, :LOW], spec[: 2 * K1, LOW:]
        right_re, right_im = spec[2 * K1 :, :LOW], spec[2 * K1 :, LOW:]
        line[: 2 * K1, :LOW] = (left_re * right_re - left_im * right_im).astype(jnp.bfloat16)
        line[: 2 * K1, LOW:] = (left_re * right_im + left_im * right_re).astype(jnp.bfloat16)
        spec[: 2 * K1, :] = dot(line[: 2 * K1, :], back[...])
        columns_re, columns_im = [], []
        for own in range(2):
            real = spec[own * K1 : (own + 1) * K1, :LOW]
            imag = spec[own * K1 : (own + 1) * K1, LOW:]
            turned_re = real * cosine - imag * sine
            turned_im = (imag * cosine + real * sine)[:N1]
            row = lax.broadcasted_iota(jnp.int32, (N1, LOW), 0)
            turned_im = jnp.where(row == 0, turned_re[N1 : N1 + 1], turned_im)
            columns_re.append(turned_re[:N1].astype(jnp.bfloat16))
            columns_im.append(turned_im.astype(jnp.bfloat16))
        result = dot(last_re[...], jnp.concatenate(columns_re, axis=1))
        result += dot(last_im[...], jnp.concatenate(columns_im, axis=1))
        result = jnp.stack(
            [result[:, own * LOW : (own + 1) * LOW].reshape(N_DEV, HIGH, LOW) for own in range(2)],
            axis=1,
        )
        send_out[half] = result.reshape(N_DEV, 2 * HIGH, LOW).astype(jnp.bfloat16)

    loads[0].wait()
    pack(filter_ref, LOW)
    loads[1].wait()
    pack(values_ref, 0)
    pl.semaphore_wait(barrier, N_DEV - 1)
    for half in range(2):
        send_all(send_in, recv_in, half, half)
    for load in loads[2:]:
        load.wait()
    for half in range(2):
        wait_all(recv_in, half, recv_sem.at[half])
        convolve(half)
        send_all(send_out, recv_out, half, 2 + half)
    for half in range(2):
        wait_all(recv_out, half, recv_sem.at[2 + half])
        wide[half] = recv_out[half].reshape(N_DEV * 2 * HIGH, LOW).astype(jnp.float32)
    for high in range(HIGH):
        turned = jnp.concatenate(
            [
                wide[own // 2, pl.ds((own % 2) * HIGH + high, N_DEV, stride=2 * HIGH), :]
                for own in range(OWN)
            ],
            axis=0,
        ).T
        out_ref[high * LOW : (high + 1) * LOW, :] = turned.astype(jnp.bfloat16)
    for half in range(2):
        wait_all(send_in, half, send_sem.at[half])
        wait_all(send_out, half, send_sem.at[2 + half])


def body(values, long_filter, skip_gain):
    operands = (long_filter, values, *(jnp.asarray(t) for t in tables()))
    convolved = pl.pallas_call(
        kernel,
        out_shape=jax.ShapeDtypeStruct(values.shape, jnp.bfloat16),
        in_specs=[pl.BlockSpec(memory_space=pltpu.HBM)] * len(operands),
        out_specs=pl.BlockSpec(memory_space=pltpu.VMEM),
        scratch_shapes=[
            *(pltpu.VMEM(x.shape, x.dtype) for x in operands),
            pltpu.SemaphoreType.DMA((len(operands),)),
            pltpu.VMEM((2, N_DEV * 2 * HIGH, LOW), jnp.float32),
            pltpu.VMEM((2, N_DEV, 2 * HIGH, 2 * LOW), jnp.bfloat16),
            pltpu.VMEM((2, N_DEV, 2 * HIGH, 2 * LOW), jnp.bfloat16),
            pltpu.VMEM((2, N_DEV, 2 * HIGH, LOW), jnp.bfloat16),
            pltpu.VMEM((2, N_DEV, 2 * HIGH, LOW), jnp.bfloat16),
            pltpu.VMEM((OWN * K1, 2 * LOW), jnp.bfloat16),
            pltpu.VMEM((OWN * K1, 2 * LOW), jnp.float32),
            pltpu.SemaphoreType.DMA((4,)),
            pltpu.SemaphoreType.DMA((4,)),
        ],
        compiler_params=pltpu.CompilerParams(
            collective_id=0, has_side_effects=True, vmem_limit_bytes=107 * 2**19
        ),
    )(*operands)
    direct = skip_gain[None, :] * values.astype(jnp.float32)
    return (convolved.astype(jnp.float32) + direct).astype(jnp.bfloat16)


def solution(mesh):
    return jax.shard_map(
        body,
        mesh=mesh,
        in_specs=(P("context", "tensor"), P("context", "tensor"), P("tensor")),
        out_specs=P("context", "tensor"),
        check_vma=False,
    )
```

```python
import math

import jax
import jax.numpy as jnp
import ml_dtypes
import numpy as np
from jax import lax
from jax.experimental import pallas as pl
from jax.experimental.pallas import tpu as pltpu
from jax.sharding import PartitionSpec as P

MESH = pl.DeviceIdType.MESH

N_DEV = 32
BLOCK = 1024
OWN = 4
HIGH, LOW = 8, 128
L1, L2 = 512, 128
N1 = L1 // 2
K1 = 272


def tables():
    length = L1 * L2
    k1 = np.arange(K1)
    n1 = np.arange(N1)
    n2 = np.arange(L2)
    kept = (k1 <= N1).astype(np.float64)[:, None]
    angle = 2 * math.pi * ((k1[:, None] * n1[None, :]) % L1) / L1
    first = np.concatenate([np.cos(angle) * kept, -np.sin(angle) * kept], axis=0)
    twist = 2 * math.pi * ((k1[:, None] * n2[None, :]) % length) / length
    angle = 2 * math.pi * ((n2[:, None] * n2[None, :]) % L2) / L2
    cosine, sine = np.cos(angle), np.sin(angle)
    second = np.block([[cosine, -sine], [sine, cosine]])
    back = np.block([[cosine, sine], [-sine, cosine]])
    k1 = np.arange(N1)
    angle = 2 * math.pi * ((n1[:, None] * k1[None, :]) % L1) / L1
    real = np.where(k1 == 0, 1.0, 2.0)[None, :] * np.cos(angle)
    imag = np.where(k1 == 0, (1.0 - 2.0 * (n1 % 2))[:, None], -2.0 * np.sin(angle))
    last = np.concatenate([real, imag], axis=1) / length
    matrices = np.concatenate([first, second, back, last[:, :N1], last[:, N1:]], axis=0)
    twists = np.concatenate([np.cos(twist), np.sin(twist)], axis=0)
    return matrices.astype(ml_dtypes.bfloat16), twists.astype(np.float32)


def dot(left, right):
    return jnp.dot(left, right, preferred_element_type=jnp.float32)


def partner(me, k):
    turn, along_y = k // 4, lax.rem(k + 1, 4)
    along_z = 4 + (1 - 2 * lax.rem(turn, 2)) * ((turn + 1) // 2)
    y, z = me // 8, lax.rem(me, 8)
    return lax.rem(y + along_y, 4) * 8 + lax.rem(z + along_z, 8)


def kernel(
    filter_hbm,
    values_hbm,
    matrices_hbm,
    twists_hbm,
    out_ref,
    filter_ref,
    values_ref,
    matrices_ref,
    twists_ref,
    load_sem,
    wide,
    send_in,
    recv_in,
    send_out,
    recv_out,
    send_sem,
    recv_sem,
):
    me = lax.axis_index("context")
    barrier = pltpu.get_barrier_semaphore()
    pairs = [
        (filter_hbm, filter_ref),
        (values_hbm, values_ref),
        (matrices_hbm, matrices_ref),
        (twists_hbm, twists_ref),
    ]
    loads = [
        pltpu.make_async_copy(source, target, load_sem.at[i])
        for i, (source, target) in enumerate(pairs)
    ]
    for load in loads:
        load.start()
    for k in range(N_DEV - 1):
        pl.semaphore_signal(
            barrier, inc=1, device_id={"context": partner(me, k)}, device_id_type=MESH
        )

    rows = [0, 2 * K1, 2 * K1 + 2 * LOW, 2 * K1 + 4 * LOW, 2 * K1 + 4 * LOW + N1]
    first, second, back, last_re, last_im = (
        matrices_ref.at[pl.ds(start, size)]
        for start, size in zip(rows, [2 * K1, 2 * LOW, 2 * LOW, N1, N1])
    )
    cos_ref, sin_ref = twists_ref.at[pl.ds(0, K1)], twists_ref.at[pl.ds(K1, K1)]

    def pack(source, lanes):
        for high in range(HIGH):
            turned = source[high * LOW : (high + 1) * LOW, :].astype(jnp.float32).T
            for own in range(OWN):
                wide[own // 2, pl.ds((own % 2) * HIGH + high, N_DEV, stride=2 * HIGH), :] = turned[
                    own * N_DEV : (own + 1) * N_DEV, :
                ]
        for half in range(2):
            send_in[half, :, :, lanes : lanes + LOW] = (
                wide[half].astype(jnp.bfloat16).reshape(N_DEV, 2 * HIGH, LOW)
            )

    def send_all(source, target, half, sem):
        for k in range(N_DEV - 1):
            device = partner(me, k)
            pltpu.make_async_remote_copy(
                src_ref=source.at[half, device],
                dst_ref=target.at[half, me],
                send_sem=send_sem.at[sem],
                recv_sem=recv_sem.at[sem],
                device_id={"context": device},
                device_id_type=MESH,
            ).start()
        target[half, me] = source[half, me]

    def send_back(half):
        y, z = me // 8, lax.rem(me, 8)
        for k in range(N_DEV):
            to_z, turn = k // 4, (k + 1) % 4
            device = lax.rem(y + turn, 4) * 8 + to_z
            copy = pltpu.make_async_remote_copy(
                src_ref=send_out.at[half, device],
                dst_ref=recv_out.at[half, me],
                send_sem=send_sem.at[2 + half],
                recv_sem=recv_sem.at[2 + half],
                device_id={"context": device},
                device_id_type=MESH,
            )
            if turn:
                copy.start()
            else:
                pl.when(z != to_z)(copy.start)
        recv_out[half, me] = send_out[half, me]

    def wait_all(buffer, half, sem):
        blocks = buffer.at[half, pl.ds(0, N_DEV - 1)]
        pltpu.make_async_copy(blocks, blocks, sem).wait()

    def convolve(half):
        rows = recv_in[half].reshape(N_DEV * 2 * HIGH, 2 * LOW).astype(jnp.float32)
        rows = rows.reshape(N_DEV, 2, HIGH, 2 * LOW)
        cosine, sine = cos_ref[...], sin_ref[...]
        row = lax.broadcasted_iota(jnp.int32, (N1, LOW), 0)
        columns_re, columns_im = [], []
        lines = []
        for own in range(2):
            part = rows[:, own].reshape(N1, 2 * LOW).astype(jnp.bfloat16)
            summed_re, summed_im = dot(first[:K1, :], part), dot(first[K1:, :], part)
            for array in range(2):
                real = summed_re[:, array * LOW : (array + 1) * LOW]
                imag = summed_im[:, array * LOW : (array + 1) * LOW]
                lines.append(jnp.concatenate(
                    [
                        (real * cosine + imag * sine).astype(jnp.bfloat16),
                        (imag * cosine - real * sine).astype(jnp.bfloat16),
                    ],
                    axis=1,
                ))
        spectra = [dot(l, second[...]) for l in lines]
        products = []
        for own in range(2):
            left_re, left_im = spectra[2*own][:, :LOW], spectra[2*own][:, LOW:]
            right_re, right_im = spectra[2*own+1][:, :LOW], spectra[2*own+1][:, LOW:]
            products.append(jnp.concatenate(
                [
                    (left_re * right_re - left_im * right_im).astype(jnp.bfloat16),
                    (left_re * right_im + left_im * right_re).astype(jnp.bfloat16),
                ],
                axis=1,
            ))
        turneds = [dot(p, back[...]) for p in products]
        for own in range(2):
            turned = turneds[own]
            real, imag = turned[:, :LOW], turned[:, LOW:]
            turned_re = real * cosine - imag * sine
            turned_im = (imag * cosine + real * sine)[:N1]
            turned_im = jnp.where(row == 0, turned_re[N1 : N1 + 1], turned_im)
            columns_re.append(turned_re[:N1].astype(jnp.bfloat16))
            columns_im.append(turned_im.astype(jnp.bfloat16))
        result = dot(
            jnp.concatenate([last_re[...], last_im[...]], axis=1),
            jnp.concatenate(
                [jnp.concatenate(columns_re, axis=1), jnp.concatenate(columns_im, axis=1)], axis=0
            ),
        )
        result = jnp.stack(
            [result[:, own * LOW : (own + 1) * LOW].reshape(N_DEV, HIGH, LOW) for own in range(2)],
            axis=1,
        )
        send_out[half] = result.reshape(N_DEV, 2 * HIGH, LOW).astype(jnp.bfloat16)

    loads[0].wait()
    pack(filter_ref, LOW)
    loads[1].wait()
    pack(values_ref, 0)
    pl.semaphore_wait(barrier, N_DEV - 1)
    for half in range(2):
        send_all(send_in, recv_in, half, half)
    for load in loads[2:]:
        load.wait()
    for half in range(2):
        wait_all(recv_in, half, recv_sem.at[half])
        convolve(half)
        send_back(half)
    for half in range(2):
        wait_all(recv_out, half, recv_sem.at[2 + half])
        wide[half] = recv_out[half].reshape(N_DEV * 2 * HIGH, LOW).astype(jnp.float32)
    for high in range(HIGH):
        turned = jnp.concatenate(
            [
                wide[own // 2, pl.ds((own % 2) * HIGH + high, N_DEV, stride=2 * HIGH), :]
                for own in range(OWN)
            ],
            axis=0,
        ).T
        out_ref[high * LOW : (high + 1) * LOW, :] = turned.astype(jnp.bfloat16)
    for half in range(2):
        wait_all(send_in, half, send_sem.at[half])
        wait_all(send_out, half, send_sem.at[2 + half])


def body(values, long_filter, skip_gain):
    operands = (long_filter, values, *(jnp.asarray(t) for t in tables()))
    convolved = pl.pallas_call(
        kernel,
        out_shape=jax.ShapeDtypeStruct(values.shape, jnp.bfloat16),
        in_specs=[pl.BlockSpec(memory_space=pltpu.HBM)] * len(operands),
        out_specs=pl.BlockSpec(memory_space=pltpu.VMEM),
        scratch_shapes=[
            *(pltpu.VMEM(x.shape, x.dtype) for x in operands),
            pltpu.SemaphoreType.DMA((len(operands),)),
            pltpu.VMEM((2, N_DEV * 2 * HIGH, LOW), jnp.float32),
            pltpu.VMEM((2, N_DEV, 2 * HIGH, 2 * LOW), jnp.bfloat16),
            pltpu.VMEM((2, N_DEV, 2 * HIGH, 2 * LOW), jnp.bfloat16),
            pltpu.VMEM((2, N_DEV, 2 * HIGH, LOW), jnp.bfloat16),
            pltpu.VMEM((2, N_DEV, 2 * HIGH, LOW), jnp.bfloat16),
            pltpu.SemaphoreType.DMA((4,)),
            pltpu.SemaphoreType.DMA((4,)),
        ],
        compiler_params=pltpu.CompilerParams(
            collective_id=0, has_side_effects=True, vmem_limit_bytes=107 * 2**19
        ),
    )(*operands)
    direct = skip_gain[None, :] * values.astype(jnp.float32)
    return (convolved.astype(jnp.float32) + direct).astype(jnp.bfloat16)


def solution(mesh):
    return jax.shard_map(
        body,
        mesh=mesh,
        in_specs=(P("context", "tensor"), P("context", "tensor"), P("tensor")),
        out_specs=P("context", "tensor"),
        check_vma=False,
    )
```

```python
import math

import jax
import jax.numpy as jnp
import ml_dtypes
import numpy as np
from jax import lax
from jax.experimental import pallas as pl
from jax.experimental.pallas import tpu as pltpu
from jax.sharding import PartitionSpec as P

MESH = pl.DeviceIdType.MESH

N_DEV = 32
BLOCK = 1024
OWN = 4
HIGH, LOW = 8, 128
L1, L2 = 512, 128
N1 = L1 // 2
FAR_FIRST = [(y, z) for z in (4, 3, 5, 2, 6, 1, 7, 0) for y in (1, 2, 3, 0) if (y, z) != (0, 0)]
MIXED = [(y, z) for y in (2, 1, 3, 0) for z in (3, 5, 2, 6, 4, 1, 7, 0) if (y, z) != (0, 0)]
K1 = 272


def tables():
    length = L1 * L2
    k1 = np.arange(K1)
    n1 = np.arange(N1)
    n2 = np.arange(L2)
    kept = (k1 <= N1).astype(np.float64)[:, None]
    angle = 2 * math.pi * ((k1[:, None] * n1[None, :]) % L1) / L1
    first = np.concatenate([np.cos(angle) * kept, -np.sin(angle) * kept], axis=0)
    twist = 2 * math.pi * ((k1[:, None] * n2[None, :]) % length) / length
    angle = 2 * math.pi * ((n2[:, None] * n2[None, :]) % L2) / L2
    cosine, sine = np.cos(angle), np.sin(angle)
    second = np.block([[cosine, -sine], [sine, cosine]])
    back = np.block([[cosine, sine], [-sine, cosine]])
    k1 = np.arange(N1)
    angle = 2 * math.pi * ((n1[:, None] * k1[None, :]) % L1) / L1
    real = np.where(k1 == 0, 1.0, 2.0)[None, :] * np.cos(angle)
    imag = np.where(k1 == 0, (1.0 - 2.0 * (n1 % 2))[:, None], -2.0 * np.sin(angle))
    last = np.concatenate([real, imag], axis=1) / length
    matrices = np.concatenate([first, second, back, last[:, :N1], last[:, N1:]], axis=0)
    twists = np.concatenate([np.cos(twist), np.sin(twist)], axis=0)
    return matrices.astype(ml_dtypes.bfloat16), twists.astype(np.float32)


def dot(left, right):
    return jnp.dot(left, right, preferred_element_type=jnp.float32)


def kernel(
    filter_hbm,
    values_hbm,
    matrices_hbm,
    twists_hbm,
    out_ref,
    filter_ref,
    values_ref,
    matrices_ref,
    twists_ref,
    load_sem,
    wide,
    send_in,
    recv_in,
    send_out,
    recv_out,
    send_sem,
    recv_sem,
):
    me = lax.axis_index("context")
    my_y, my_z = me // 8, lax.rem(me, 8)
    barrier = pltpu.get_barrier_semaphore()

    def partner(steps):
        return lax.rem(my_y + steps[0], 4) * 8 + lax.rem(my_z + steps[1], 8)

    pairs = [
        (filter_hbm, filter_ref),
        (values_hbm, values_ref),
        (matrices_hbm, matrices_ref),
        (twists_hbm, twists_ref),
    ]
    loads = [
        pltpu.make_async_copy(source, target, load_sem.at[i])
        for i, (source, target) in enumerate(pairs)
    ]
    loads[0].start()
    for steps in FAR_FIRST:
        pl.semaphore_signal(
            barrier, inc=1, device_id={"context": partner(steps)}, device_id_type=MESH
        )
    for load in loads[1:]:
        load.start()

    rows = [0, 2 * K1, 2 * K1 + 2 * LOW, 2 * K1 + 4 * LOW, 2 * K1 + 4 * LOW + N1]
    first, second, back, last_re, last_im = (
        matrices_ref.at[pl.ds(start, size)]
        for start, size in zip(rows, [2 * K1, 2 * LOW, 2 * LOW, N1, N1])
    )
    cos_ref, sin_ref = twists_ref.at[pl.ds(0, K1)], twists_ref.at[pl.ds(K1, K1)]

    def pack(source, lanes):
        for high in range(HIGH):
            turned = source[high * LOW : (high + 1) * LOW, :].astype(jnp.float32).T
            for own in range(OWN):
                wide[own // 2, pl.ds((own % 2) * HIGH + high, N_DEV, stride=2 * HIGH), :] = turned[
                    own * N_DEV : (own + 1) * N_DEV, :
                ]
        for half in range(2):
            send_in[half, :, :, lanes : lanes + LOW] = (
                wide[half].astype(jnp.bfloat16).reshape(N_DEV, 2 * HIGH, LOW)
            )

    def copy_to(source, target, half, sem, device):
        return pltpu.make_async_remote_copy(
            src_ref=source.at[half, device],
            dst_ref=target.at[half, me],
            send_sem=send_sem.at[sem],
            recv_sem=recv_sem.at[sem],
            device_id={"context": device},
            device_id_type=MESH,
        )

    def send_blocks(half):
        for steps in MIXED:
            copy_to(send_in, recv_in, half, half, partner(steps)).start()
        recv_in[half, me] = send_in[half, me]

    def send_back(half):
        for k in range(N_DEV):
            to_z, turn = k // 4, (k + 1) % 4
            device = lax.rem(my_y + turn, 4) * 8 + to_z
            copy = copy_to(send_out, recv_out, half, 2 + half, device)
            if turn:
                copy.start()
            else:
                pl.when(my_z != to_z)(copy.start)
        recv_out[half, me] = send_out[half, me]

    def wait_all(buffer, half, sem):
        blocks = buffer.at[half, pl.ds(0, N_DEV - 1)]
        pltpu.make_async_copy(blocks, blocks, sem).wait()

    def convolve(half):
        rows = recv_in[half].reshape(N_DEV * 2 * HIGH, 2 * LOW).astype(jnp.float32)
        rows = rows.reshape(N_DEV, 2, HIGH, 2 * LOW)
        cosine, sine = cos_ref[...], sin_ref[...]
        row = lax.broadcasted_iota(jnp.int32, (N1, LOW), 0)
        columns_re, columns_im = [], []
        lines = []
        for own in range(2):
            part = rows[:, own].reshape(N1, 2 * LOW).astype(jnp.bfloat16)
            summed_re, summed_im = dot(first[:K1, :], part), dot(first[K1:, :], part)
            for array in range(2):
                real = summed_re[:, array * LOW : (array + 1) * LOW]
                imag = summed_im[:, array * LOW : (array + 1) * LOW]
                lines.append(jnp.concatenate(
                    [
                        (real * cosine + imag * sine).astype(jnp.bfloat16),
                        (imag * cosine - real * sine).astype(jnp.bfloat16),
                    ],
                    axis=1,
                ))
        spectra = [dot(l, second[...]) for l in lines]
        products = []
        for own in range(2):
            left_re, left_im = spectra[2*own][:, :LOW], spectra[2*own][:, LOW:]
            right_re, right_im = spectra[2*own+1][:, :LOW], spectra[2*own+1][:, LOW:]
            products.append(jnp.concatenate(
                [
                    (left_re * right_re - left_im * right_im).astype(jnp.bfloat16),
                    (left_re * right_im + left_im * right_re).astype(jnp.bfloat16),
                ],
                axis=1,
            ))
        turneds = [dot(p, back[...]) for p in products]
        for own in range(2):
            turned = turneds[own]
            real, imag = turned[:, :LOW], turned[:, LOW:]
            turned_re = real * cosine - imag * sine
            turned_im = (imag * cosine + real * sine)[:N1]
            turned_im = jnp.where(row == 0, turned_re[N1 : N1 + 1], turned_im)
            columns_re.append(turned_re[:N1].astype(jnp.bfloat16))
            columns_im.append(turned_im.astype(jnp.bfloat16))
        result = dot(
            jnp.concatenate([last_re[...], last_im[...]], axis=1),
            jnp.concatenate(
                [jnp.concatenate(columns_re, axis=1), jnp.concatenate(columns_im, axis=1)], axis=0
            ),
        )
        result = jnp.stack(
            [result[:, own * LOW : (own + 1) * LOW].reshape(N_DEV, HIGH, LOW) for own in range(2)],
            axis=1,
        )
        send_out[half] = result.reshape(N_DEV, 2 * HIGH, LOW).astype(jnp.bfloat16)

    loads[0].wait()
    pack(filter_ref, LOW)
    loads[1].wait()
    pack(values_ref, 0)
    pl.semaphore_wait(barrier, N_DEV - 1)
    for half in range(2):
        send_blocks(half)
    for load in loads[2:]:
        load.wait()
    for half in range(2):
        wait_all(recv_in, half, recv_sem.at[half])
        convolve(half)
        send_back(half)
    for half in range(2):
        wait_all(recv_out, half, recv_sem.at[2 + half])
        wide[half] = recv_out[half].reshape(N_DEV * 2 * HIGH, LOW).astype(jnp.float32)
    for high in range(HIGH):
        turned = jnp.concatenate(
            [
                wide[own // 2, pl.ds((own % 2) * HIGH + high, N_DEV, stride=2 * HIGH), :]
                for own in range(OWN)
            ],
            axis=0,
        ).T
        out_ref[high * LOW : (high + 1) * LOW, :] = turned.astype(jnp.bfloat16)
    for half in range(2):
        wait_all(send_in, half, send_sem.at[half])
        wait_all(send_out, half, send_sem.at[2 + half])


def body(values, long_filter, skip_gain):
    operands = (long_filter, values, *(jnp.asarray(t) for t in tables()))
    convolved = pl.pallas_call(
        kernel,
        out_shape=jax.ShapeDtypeStruct(values.shape, jnp.bfloat16),
        in_specs=[pl.BlockSpec(memory_space=pltpu.HBM)] * len(operands),
        out_specs=pl.BlockSpec(memory_space=pltpu.VMEM),
        scratch_shapes=[
            *(pltpu.VMEM(x.shape, x.dtype) for x in operands),
            pltpu.SemaphoreType.DMA((len(operands),)),
            pltpu.VMEM((2, N_DEV * 2 * HIGH, LOW), jnp.float32),
            pltpu.VMEM((2, N_DEV, 2 * HIGH, 2 * LOW), jnp.bfloat16),
            pltpu.VMEM((2, N_DEV, 2 * HIGH, 2 * LOW), jnp.bfloat16),
            pltpu.VMEM((2, N_DEV, 2 * HIGH, LOW), jnp.bfloat16),
            pltpu.VMEM((2, N_DEV, 2 * HIGH, LOW), jnp.bfloat16),
            pltpu.SemaphoreType.DMA((4,)),
            pltpu.SemaphoreType.DMA((4,)),
        ],
        compiler_params=pltpu.CompilerParams(
            collective_id=0, has_side_effects=True, vmem_limit_bytes=107 * 2**19
        ),
    )(*operands)
    direct = skip_gain[None, :] * values.astype(jnp.float32)
    return (convolved.astype(jnp.float32) + direct).astype(jnp.bfloat16)


def solution(mesh):
    return jax.shard_map(
        body,
        mesh=mesh,
        in_specs=(P("context", "tensor"), P("context", "tensor"), P("tensor")),
        out_specs=P("context", "tensor"),
        check_vma=False,
    )
```

```python
import math

import jax
import jax.numpy as jnp
import ml_dtypes
import numpy as np
from jax import lax
from jax.experimental import pallas as pl
from jax.experimental.pallas import tpu as pltpu
from jax.sharding import PartitionSpec as P

MESH = pl.DeviceIdType.MESH

N_DEV = 32
BLOCK = 1024
OWN = 4
HIGH, LOW = 8, 128
L1, L2 = 512, 128
N1 = L1 // 2
FAR_FIRST = [(y, z) for z in (4, 3, 5, 2, 6, 1, 7, 0) for y in (1, 2, 3, 0) if (y, z) != (0, 0)]
MIXED = [(y, z) for y in (2, 1, 3, 0) for z in (3, 5, 2, 6, 4, 1, 7, 0) if (y, z) != (0, 0)]
K1 = 272


def tables():
    length = L1 * L2
    k1 = np.arange(K1)
    n1 = np.arange(N1)
    n2 = np.arange(L2)
    kept = (k1 <= N1).astype(np.float64)[:, None]
    angle = 2 * math.pi * ((k1[:, None] * n1[None, :]) % L1) / L1
    first = np.concatenate([np.cos(angle) * kept, -np.sin(angle) * kept], axis=0)
    twist = 2 * math.pi * ((k1[:, None] * n2[None, :]) % length) / length
    angle = 2 * math.pi * ((n2[:, None] * n2[None, :]) % L2) / L2
    cosine, sine = np.cos(angle), np.sin(angle)
    second = np.block([[cosine, -sine], [sine, cosine]])
    back = np.block([[cosine, sine], [-sine, cosine]])
    k1 = np.arange(N1)
    angle = 2 * math.pi * ((n1[:, None] * k1[None, :]) % L1) / L1
    real = np.where(k1 == 0, 1.0, 2.0)[None, :] * np.cos(angle)
    imag = np.where(k1 == 0, (1.0 - 2.0 * (n1 % 2))[:, None], -2.0 * np.sin(angle))
    last = np.concatenate([real, imag], axis=1) / length
    matrices = np.concatenate([first, second, back, last[:, :N1], last[:, N1:]], axis=0)
    twists = np.concatenate([np.cos(twist), np.sin(twist)], axis=0)
    return matrices.astype(ml_dtypes.bfloat16), twists.astype(np.float32)


def dot(left, right):
    return jnp.dot(left, right, preferred_element_type=jnp.float32)


def kernel(
    filter_hbm,
    values_hbm,
    matrices_hbm,
    twists_hbm,
    out_ref,
    filter_ref,
    values_ref,
    matrices_ref,
    twists_ref,
    load_sem,
    wide,
    send_in,
    recv_in,
    send_out,
    recv_out,
    send_sem,
    recv_sem,
):
    me = lax.axis_index("context")
    my_y, my_z = me // 8, lax.rem(me, 8)
    barrier = pltpu.get_barrier_semaphore()

    def partner(steps):
        return lax.rem(my_y + steps[0], 4) * 8 + lax.rem(my_z + steps[1], 8)

    pairs = [
        (filter_hbm, filter_ref),
        (values_hbm, values_ref),
        (matrices_hbm, matrices_ref),
        (twists_hbm, twists_ref),
    ]
    loads = [
        pltpu.make_async_copy(source, target, load_sem.at[i])
        for i, (source, target) in enumerate(pairs)
    ]
    loads[0].start()
    for steps in FAR_FIRST:
        pl.semaphore_signal(
            barrier, inc=1, device_id={"context": partner(steps)}, device_id_type=MESH
        )
    lane = lax.axis_index("tensor")
    sibling = lane + 1 - 2 * lax.rem(lane, 2)
    pl.semaphore_signal(
        barrier, inc=1, device_id={"tensor": sibling, "context": me}, device_id_type=MESH
    )
    for load in loads[1:]:
        load.start()

    rows = [0, 2 * K1, 2 * K1 + 2 * LOW, 2 * K1 + 4 * LOW, 2 * K1 + 4 * LOW + N1]
    first, second, back, last_re, last_im = (
        matrices_ref.at[pl.ds(start, size)]
        for start, size in zip(rows, [2 * K1, 2 * LOW, 2 * LOW, N1, N1])
    )
    cos_ref, sin_ref = twists_ref.at[pl.ds(0, K1)], twists_ref.at[pl.ds(K1, K1)]

    def pack(source, lanes):
        for high in range(HIGH):
            turned = source[high * LOW : (high + 1) * LOW, :].astype(jnp.float32).T
            for own in range(OWN):
                wide[own // 2, pl.ds((own % 2) * HIGH + high, N_DEV, stride=2 * HIGH), :] = turned[
                    own * N_DEV : (own + 1) * N_DEV, :
                ]
        for half in range(2):
            send_in[half, :, :, lanes : lanes + LOW] = (
                wide[half].astype(jnp.bfloat16).reshape(N_DEV, 2 * HIGH, LOW)
            )

    def copy_to(source, target, half, sem, device):
        return pltpu.make_async_remote_copy(
            src_ref=source.at[half, device],
            dst_ref=target.at[half, me],
            send_sem=send_sem.at[sem],
            recv_sem=recv_sem.at[sem],
            device_id={"context": device},
            device_id_type=MESH,
        )

    def send_blocks(half):
        for steps in MIXED:
            copy_to(send_in, recv_in, half, half, partner(steps)).start()
        recv_in[half, me] = send_in[half, me]

    def send_back(half):
        for k in range(N_DEV):
            to_z, turn = k // 4, (k + 1) % 4
            device = lax.rem(my_y + turn, 4) * 8 + to_z
            copy = copy_to(send_out, recv_out, half, 2 + half, device)
            if turn:
                copy.start()
            else:
                pl.when(my_z != to_z)(copy.start)
        recv_out[half, me] = send_out[half, me]

    def wait_all(buffer, half, sem):
        blocks = buffer.at[half, pl.ds(0, N_DEV - 1)]
        pltpu.make_async_copy(blocks, blocks, sem).wait()

    def convolve(half):
        rows = recv_in[half].reshape(N_DEV * 2 * HIGH, 2 * LOW).astype(jnp.float32)
        rows = rows.reshape(N_DEV, 2, HIGH, 2 * LOW)
        cosine, sine = cos_ref[...], sin_ref[...]
        row = lax.broadcasted_iota(jnp.int32, (N1, LOW), 0)
        columns_re, columns_im = [], []
        lines = []
        for own in range(2):
            part = rows[:, own].reshape(N1, 2 * LOW).astype(jnp.bfloat16)
            summed_re, summed_im = dot(first[:K1, :], part), dot(first[K1:, :], part)
            for array in range(2):
                real = summed_re[:, array * LOW : (array + 1) * LOW]
                imag = summed_im[:, array * LOW : (array + 1) * LOW]
                lines.append(jnp.concatenate(
                    [
                        (real * cosine + imag * sine).astype(jnp.bfloat16),
                        (imag * cosine - real * sine).astype(jnp.bfloat16),
                    ],
                    axis=1,
                ))
        spectra = [dot(l, second[...]) for l in lines]
        products = []
        for own in range(2):
            left_re, left_im = spectra[2*own][:, :LOW], spectra[2*own][:, LOW:]
            right_re, right_im = spectra[2*own+1][:, :LOW], spectra[2*own+1][:, LOW:]
            products.append(jnp.concatenate(
                [
                    (left_re * right_re - left_im * right_im).astype(jnp.bfloat16),
                    (left_re * right_im + left_im * right_re).astype(jnp.bfloat16),
                ],
                axis=1,
            ))
        turneds = [dot(p, back[...]) for p in products]
        for own in range(2):
            turned = turneds[own]
            real, imag = turned[:, :LOW], turned[:, LOW:]
            turned_re = real * cosine - imag * sine
            turned_im = (imag * cosine + real * sine)[:N1]
            turned_im = jnp.where(row == 0, turned_re[N1 : N1 + 1], turned_im)
            columns_re.append(turned_re[:N1].astype(jnp.bfloat16))
            columns_im.append(turned_im.astype(jnp.bfloat16))
        result = dot(
            jnp.concatenate([last_re[...], last_im[...]], axis=1),
            jnp.concatenate(
                [jnp.concatenate(columns_re, axis=1), jnp.concatenate(columns_im, axis=1)], axis=0
            ),
        )
        result = jnp.stack(
            [result[:, own * LOW : (own + 1) * LOW].reshape(N_DEV, HIGH, LOW) for own in range(2)],
            axis=1,
        )
        send_out[half] = result.reshape(N_DEV, 2 * HIGH, LOW).astype(jnp.bfloat16)

    loads[0].wait()
    pack(filter_ref, LOW)
    loads[1].wait()
    pack(values_ref, 0)
    pl.semaphore_wait(barrier, N_DEV)
    for half in range(2):
        send_blocks(half)
    for load in loads[2:]:
        load.wait()
    for half in range(2):
        wait_all(recv_in, half, recv_sem.at[half])
        convolve(half)
        send_back(half)
    for half in range(2):
        wait_all(recv_out, half, recv_sem.at[2 + half])
        out_ref[half] = recv_out[half]
    for half in range(2):
        wait_all(send_in, half, send_sem.at[half])
        wait_all(send_out, half, send_sem.at[2 + half])


def finish(blocks_ref, values_ref, gain_ref, out_hbm, wide, staged, sem):
    for half in range(2):
        wide[half] = blocks_ref[half].reshape(N_DEV * 2 * HIGH, LOW).astype(jnp.float32)
    copies = []
    for high in range(HIGH):
        rows = pl.ds(high * LOW, LOW)
        turned = jnp.concatenate(
            [
                wide[own // 2, pl.ds((own % 2) * HIGH + high, N_DEV, stride=2 * HIGH), :]
                for own in range(OWN)
            ],
            axis=0,
        ).T
        direct = gain_ref[...] * values_ref[rows, :].astype(jnp.float32)
        staged[rows, :] = (turned + direct).astype(jnp.bfloat16)
        copy = pltpu.make_async_copy(staged.at[rows], out_hbm.at[rows], sem.at[high])
        copy.start()
        copies.append(copy)
    for copy in copies:
        copy.wait()


def body(values, long_filter, skip_gain):
    operands = (long_filter, values, *(jnp.asarray(t) for t in tables()))
    blocks = pl.pallas_call(
        kernel,
        out_shape=jax.ShapeDtypeStruct((2, N_DEV, 2 * HIGH, LOW), jnp.bfloat16),
        in_specs=[pl.BlockSpec(memory_space=pltpu.HBM)] * len(operands),
        out_specs=pl.BlockSpec(memory_space=pltpu.VMEM),
        scratch_shapes=[
            *(pltpu.VMEM(x.shape, x.dtype) for x in operands),
            pltpu.SemaphoreType.DMA((len(operands),)),
            pltpu.VMEM((2, N_DEV * 2 * HIGH, LOW), jnp.float32),
            pltpu.VMEM((2, N_DEV, 2 * HIGH, 2 * LOW), jnp.bfloat16),
            pltpu.VMEM((2, N_DEV, 2 * HIGH, 2 * LOW), jnp.bfloat16),
            pltpu.VMEM((2, N_DEV, 2 * HIGH, LOW), jnp.bfloat16),
            pltpu.VMEM((2, N_DEV, 2 * HIGH, LOW), jnp.bfloat16),
            pltpu.SemaphoreType.DMA((4,)),
            pltpu.SemaphoreType.DMA((4,)),
        ],
        compiler_params=pltpu.CompilerParams(
            collective_id=0, has_side_effects=True, vmem_limit_bytes=107 * 2**19
        ),
    )(*operands)
    vmem = pl.BlockSpec(memory_space=pltpu.VMEM)
    return pl.pallas_call(
        finish,
        out_shape=jax.ShapeDtypeStruct(values.shape, jnp.bfloat16),
        in_specs=[vmem] * 3,
        out_specs=pl.BlockSpec(memory_space=pltpu.HBM),
        scratch_shapes=[
            pltpu.VMEM((2, N_DEV * 2 * HIGH, LOW), jnp.float32),
            pltpu.VMEM(values.shape, jnp.bfloat16),
            pltpu.SemaphoreType.DMA((HIGH,)),
        ],
        compiler_params=pltpu.CompilerParams(vmem_limit_bytes=8 * 2**20),
    )(blocks, values, skip_gain.reshape(1, values.shape[1]))


def solution(mesh):
    return jax.shard_map(
        body,
        mesh=mesh,
        in_specs=(P("context", "tensor"), P("context", "tensor"), P("tensor")),
        out_specs=P("context", "tensor"),
        check_vma=False,
    )
```

```python
import math

import jax
import jax.numpy as jnp
import ml_dtypes
import numpy as np
from jax import lax
from jax.experimental import pallas as pl
from jax.experimental.pallas import tpu as pltpu
from jax.sharding import PartitionSpec as P

MESH = pl.DeviceIdType.MESH

N_DEV = 32
BLOCK = 1024
OWN = 4
HIGH, LOW = 8, 128
L1, L2 = 512, 128
N1 = L1 // 2
FAR_FIRST = [(y, z) for z in (4, 3, 5, 2, 6, 1, 7, 0) for y in (1, 2, 3, 0) if (y, z) != (0, 0)]
MIXED = [(y, z) for y in (2, 1, 3, 0) for z in (3, 5, 2, 6, 4, 1, 7, 0) if (y, z) != (0, 0)]
K1 = 272


def tables():
    length = L1 * L2
    k1 = np.arange(K1)
    n1 = np.arange(N1)
    n2 = np.arange(L2)
    kept = (k1 <= N1).astype(np.float64)[:, None]
    angle = 2 * math.pi * ((k1[:, None] * n1[None, :]) % L1) / L1
    first = np.concatenate([np.cos(angle) * kept, -np.sin(angle) * kept], axis=0)
    twist = 2 * math.pi * ((k1[:, None] * n2[None, :]) % length) / length
    angle = 2 * math.pi * ((n2[:, None] * n2[None, :]) % L2) / L2
    cosine, sine = np.cos(angle), np.sin(angle)
    second = np.block([[cosine, -sine], [sine, cosine]])
    back = np.block([[cosine, sine], [-sine, cosine]])
    k1 = np.arange(N1)
    angle = 2 * math.pi * ((n1[:, None] * k1[None, :]) % L1) / L1
    real = np.where(k1 == 0, 1.0, 2.0)[None, :] * np.cos(angle)
    imag = np.where(k1 == 0, (1.0 - 2.0 * (n1 % 2))[:, None], -2.0 * np.sin(angle))
    last = np.concatenate([real, imag], axis=1) / length
    matrices = np.concatenate([first, second, back, last[:, :N1], last[:, N1:]], axis=0)
    twists = np.concatenate([np.cos(twist), np.sin(twist)], axis=0)
    return matrices.astype(ml_dtypes.bfloat16), twists.astype(np.float32)


def dot(left, right):
    return jnp.dot(left, right, preferred_element_type=jnp.float32)


def kernel(
    filter_hbm,
    values_hbm,
    matrices_hbm,
    twists_hbm,
    out_ref,
    filter_ref,
    values_ref,
    matrices_ref,
    twists_ref,
    load_sem,
    wide,
    send_in,
    recv_in,
    send_out,
    recv_out,
    send_sem,
    recv_sem,
):
    me = lax.axis_index("context")
    my_y, my_z = me // 8, lax.rem(me, 8)
    barrier = pltpu.get_barrier_semaphore()

    def partner(steps):
        return lax.rem(my_y + steps[0], 4) * 8 + lax.rem(my_z + steps[1], 8)

    pairs = [
        (filter_hbm, filter_ref),
        (values_hbm, values_ref),
        (matrices_hbm, matrices_ref),
        (twists_hbm, twists_ref),
    ]
    loads = [
        pltpu.make_async_copy(source, target, load_sem.at[i])
        for i, (source, target) in enumerate(pairs)
    ]
    lane = lax.axis_index("tensor")
    sibling = lane + 1 - 2 * lax.rem(lane, 2)
    pl.semaphore_signal(
        barrier, inc=1, device_id={"tensor": sibling, "context": me}, device_id_type=MESH
    )
    for steps in FAR_FIRST:
        pl.semaphore_signal(
            barrier, inc=1, device_id={"context": partner(steps)}, device_id_type=MESH
        )
    for load in loads:
        load.start()

    rows = [0, 2 * K1, 2 * K1 + 2 * LOW, 2 * K1 + 4 * LOW, 2 * K1 + 4 * LOW + N1]
    first, second, back, last_re, last_im = (
        matrices_ref.at[pl.ds(start, size)]
        for start, size in zip(rows, [2 * K1, 2 * LOW, 2 * LOW, N1, N1])
    )
    cos_ref, sin_ref = twists_ref.at[pl.ds(0, K1)], twists_ref.at[pl.ds(K1, K1)]

    def pack(source, lanes):
        for high in range(HIGH):
            turned = source[high * LOW : (high + 1) * LOW, :].astype(jnp.float32).T
            for own in range(OWN):
                wide[own // 2, pl.ds((own % 2) * HIGH + high, N_DEV, stride=2 * HIGH), :] = turned[
                    own * N_DEV : (own + 1) * N_DEV, :
                ]
        for half in range(2):
            send_in[half, :, :, lanes : lanes + LOW] = (
                wide[half].astype(jnp.bfloat16).reshape(N_DEV, 2 * HIGH, LOW)
            )

    def copy_to(source, target, half, sem, device):
        return pltpu.make_async_remote_copy(
            src_ref=source.at[half, device],
            dst_ref=target.at[half, me],
            send_sem=send_sem.at[sem],
            recv_sem=recv_sem.at[sem],
            device_id={"context": device},
            device_id_type=MESH,
        )

    def send_blocks(half):
        for steps in MIXED:
            copy_to(send_in, recv_in, half, half, partner(steps)).start()
        recv_in[half, me] = send_in[half, me]

    def send_back(half):
        for k in range(N_DEV):
            to_z, turn = k // 4, (k + 1) % 4
            device = lax.rem(my_y + turn, 4) * 8 + to_z
            copy = copy_to(send_out, recv_out, half, 2 + half, device)
            if turn:
                copy.start()
            else:
                pl.when(my_z != to_z)(copy.start)
        recv_out[half, me] = send_out[half, me]

    def wait_all(buffer, half, sem):
        blocks = buffer.at[half, pl.ds(0, N_DEV - 1)]
        pltpu.make_async_copy(blocks, blocks, sem).wait()

    def convolve(half):
        rows = recv_in[half].reshape(N_DEV * 2 * HIGH, 2 * LOW).astype(jnp.float32)
        rows = rows.reshape(N_DEV, 2, HIGH, 2 * LOW)
        cosine, sine = cos_ref[...], sin_ref[...]
        row = lax.broadcasted_iota(jnp.int32, (N1, LOW), 0)
        columns_re, columns_im = [], []
        lines = []
        for own in range(2):
            part = rows[:, own].reshape(N1, 2 * LOW).astype(jnp.bfloat16)
            summed_re, summed_im = dot(first[:K1, :], part), dot(first[K1:, :], part)
            for array in range(2):
                real = summed_re[:, array * LOW : (array + 1) * LOW]
                imag = summed_im[:, array * LOW : (array + 1) * LOW]
                lines.append(jnp.concatenate(
                    [
                        (real * cosine + imag * sine).astype(jnp.bfloat16),
                        (imag * cosine - real * sine).astype(jnp.bfloat16),
                    ],
                    axis=1,
                ))
        spectra = [dot(l, second[...]) for l in lines]
        products = []
        for own in range(2):
            left_re, left_im = spectra[2*own][:, :LOW], spectra[2*own][:, LOW:]
            right_re, right_im = spectra[2*own+1][:, :LOW], spectra[2*own+1][:, LOW:]
            products.append(jnp.concatenate(
                [
                    (left_re * right_re - left_im * right_im).astype(jnp.bfloat16),
                    (left_re * right_im + left_im * right_re).astype(jnp.bfloat16),
                ],
                axis=1,
            ))
        turneds = [dot(p, back[...]) for p in products]
        for own in range(2):
            turned = turneds[own]
            real, imag = turned[:, :LOW], turned[:, LOW:]
            turned_re = real * cosine - imag * sine
            turned_im = (imag * cosine + real * sine)[:N1]
            turned_im = jnp.where(row == 0, turned_re[N1 : N1 + 1], turned_im)
            columns_re.append(turned_re[:N1].astype(jnp.bfloat16))
            columns_im.append(turned_im.astype(jnp.bfloat16))
        result = dot(
            jnp.concatenate([last_re[...], last_im[...]], axis=1),
            jnp.concatenate(
                [jnp.concatenate(columns_re, axis=1), jnp.concatenate(columns_im, axis=1)], axis=0
            ),
        )
        result = jnp.stack(
            [result[:, own * LOW : (own + 1) * LOW].reshape(N_DEV, HIGH, LOW) for own in range(2)],
            axis=1,
        )
        send_out[half] = result.reshape(N_DEV, 2 * HIGH, LOW).astype(jnp.bfloat16)

    loads[0].wait()
    pack(filter_ref, LOW)
    loads[1].wait()
    pack(values_ref, 0)
    pl.semaphore_wait(barrier, N_DEV)
    for half in range(2):
        send_blocks(half)
    for load in loads[2:]:
        load.wait()
    for half in range(2):
        wait_all(recv_in, half, recv_sem.at[half])
        convolve(half)
        send_back(half)
    for half in range(2):
        wait_all(recv_out, half, recv_sem.at[2 + half])
        out_ref[half] = recv_out[half]
    for half in range(2):
        wait_all(send_in, half, send_sem.at[half])
        wait_all(send_out, half, send_sem.at[2 + half])


def finish(blocks_ref, values_ref, gain_ref, out_hbm, wide, staged, sem):
    for half in range(2):
        wide[half] = blocks_ref[half].reshape(N_DEV * 2 * HIGH, LOW).astype(jnp.float32)
    copies = []
    for high in range(HIGH):
        rows = pl.ds(high * LOW, LOW)
        turned = jnp.concatenate(
            [
                wide[own // 2, pl.ds((own % 2) * HIGH + high, N_DEV, stride=2 * HIGH), :]
                for own in range(OWN)
            ],
            axis=0,
        ).T
        direct = gain_ref[...] * values_ref[rows, :].astype(jnp.float32)
        staged[rows, :] = (turned + direct).astype(jnp.bfloat16)
        copy = pltpu.make_async_copy(staged.at[rows], out_hbm.at[rows], sem.at[high])
        copy.start()
        copies.append(copy)
    for copy in copies:
        copy.wait()


def body(values, long_filter, skip_gain):
    operands = (long_filter, values, *(jnp.asarray(t) for t in tables()))
    blocks = pl.pallas_call(
        kernel,
        out_shape=jax.ShapeDtypeStruct((2, N_DEV, 2 * HIGH, LOW), jnp.bfloat16),
        in_specs=[pl.BlockSpec(memory_space=pltpu.HBM)] * len(operands),
        out_specs=pl.BlockSpec(memory_space=pltpu.VMEM),
        scratch_shapes=[
            *(pltpu.VMEM(x.shape, x.dtype) for x in operands),
            pltpu.SemaphoreType.DMA((len(operands),)),
            pltpu.VMEM((2, N_DEV * 2 * HIGH, LOW), jnp.float32),
            pltpu.VMEM((2, N_DEV, 2 * HIGH, 2 * LOW), jnp.bfloat16),
            pltpu.VMEM((2, N_DEV, 2 * HIGH, 2 * LOW), jnp.bfloat16),
            pltpu.VMEM((2, N_DEV, 2 * HIGH, LOW), jnp.bfloat16),
            pltpu.VMEM((2, N_DEV, 2 * HIGH, LOW), jnp.bfloat16),
            pltpu.SemaphoreType.DMA((4,)),
            pltpu.SemaphoreType.DMA((4,)),
        ],
        compiler_params=pltpu.CompilerParams(
            collective_id=0, has_side_effects=True, vmem_limit_bytes=107 * 2**19
        ),
    )(*operands)
    vmem = pl.BlockSpec(memory_space=pltpu.VMEM)
    return pl.pallas_call(
        finish,
        out_shape=jax.ShapeDtypeStruct(values.shape, jnp.bfloat16),
        in_specs=[vmem] * 3,
        out_specs=pl.BlockSpec(memory_space=pltpu.HBM),
        scratch_shapes=[
            pltpu.VMEM((2, N_DEV * 2 * HIGH, LOW), jnp.float32),
            pltpu.VMEM(values.shape, jnp.bfloat16),
            pltpu.SemaphoreType.DMA((HIGH,)),
        ],
        compiler_params=pltpu.CompilerParams(vmem_limit_bytes=8 * 2**20),
    )(blocks, values, skip_gain.reshape(1, values.shape[1]))


def solution(mesh):
    return jax.shard_map(
        body,
        mesh=mesh,
        in_specs=(P("context", "tensor"), P("context", "tensor"), P("tensor")),
        out_specs=P("context", "tensor"),
        check_vma=False,
    )
```
